32 devices in a mesh: peel: 2 (over x), tile: 16 (over z, y, core).
Axes of the slice: x: 2, y: 2, z: 4, core: 2. Of those that a mesh axis runs over, the one named last changes fastest.
Arguments:
- season_ids: int32 [16], P('peel'), parts along dimension 0, may hold values from 0 to 23
- season_table: float32 [5, 24], replicated, may hold values from 0.5 to 2
- shelf_mask: int32 [128, 1024], P('tile'), may hold values 0 or 1
- codes: int32 [128, 1024], P('tile'), may hold values from 0 to 3
- spawn: float32 [128, 1024], P('tile'), may hold values from 0.2 to 5
- survey: float32 [4, 128, 1024], P('peel', 'tile'), parts along dimension 0, may hold values from 0.2 to 2
Outputs:
- concentration: float32 [16, 128, 1024], P('peel', 'tile'), parts along dimension 0
- adjoint: float32 [16, 128, 1024], P('peel', 'tile'), parts along dimension 0
- gradient: float32 [128, 2048], P('tile', 'peel'), parts along dimension 1
The draws below stay inside these ranges and needn't reach their ends.
There are 2 independent parts, one for each index of `peel`. The reference program is written for one: setup_inputs(seed, part) draws one part's arguments, and reference() takes and returns one part's arrays. A program takes and returns all parts, laid end to end along the dimension named above; an argument that names none is the same for every part. Nothing has to cross between parts.
Inputs may be any that keep to these rules, and one draw needn't show every extreme that they name: `season_ids`: seasons may repeat within a peel. `codes`: bit 0 of a code picks the upwind neighbour along the first dimension (0: the lower index), bit 1 along the second.
All inputs are finite; a program needn't handle non-finite values. No bound on the sum of `shelf_mask` on one device may be relied on, other than what follows from the above.
Results may differ from the reference program's by a relative error of at most 0.0003.
Values sent between devices are 32-bit elements; how exact they have to be, the bound alone decides.
A program may use at most 64 MiB of HBM per device.

```python
import math
import jax
import jax.numpy as jnp

NY = 1024
SEASONS = 8
ALL_SEASONS = 24
CYCLES = 2
LEVELS = 3
COARSE_SWEEPS = 8
NX = 128


def touch_ends(drawn, own_key, low, top_value):
    extent = drawn.shape
    index_at = [jax.random.randint(jax.random.fold_in(own_key, axis), (), 0, extent[axis]) for axis in range(len(extent))]
    drawn = drawn.at[tuple(index_at)].set(low)
    longest = extent.index(max(extent))
    index_at[longest] = (index_at[longest] + 1) % extent[longest]
    return drawn.at[tuple(index_at)].set(top_value)


def steps_of(own_key, shape, split, low, high):
    def one(position, blocks):
        draws = jax.random.uniform(jax.random.fold_in(jax.random.fold_in(own_key, 6), position), (blocks,), jnp.float32, low / len(split), high / len(split))
        return jnp.repeat(jnp.exp(draws), shape[position] // blocks).reshape((-1,) + (1,) * (len(shape) - position - 1))

    factor_of = one(*split[0])
    for cut in split[1:]:
        factor_of = factor_of * one(*cut)
    return factor_of


def setup_inputs(seed: int = 0, part: int = 0) -> dict:
    arg_keys = jax.random.split(jax.random.key(seed), 7)
    part_splits = jax.random.split(jax.random.fold_in(arg_keys[6], part), 7)
    season_ids = touch_ends(jax.random.randint(part_splits[0], (SEASONS,), 0, ALL_SEASONS), jax.random.fold_in(part_splits[0], 1), 0, ALL_SEASONS - 1).astype(jnp.int32)
    season_table = jnp.clip(jax.random.uniform(arg_keys[1], (5, ALL_SEASONS), jnp.float32, 0.5, 2.0), 0.5, 2.0)
    shelf_mask = touch_ends((jax.random.randint(arg_keys[2], (NX, NY), 0, 8) < 7).astype(jnp.int32), jax.random.fold_in(arg_keys[2], 1), 0, 1)
    codes = touch_ends(jax.random.randint(arg_keys[3], (NX, NY), 0, 4), jax.random.fold_in(arg_keys[3], 1), 0, 3).astype(jnp.int32)
    spawn = jnp.clip(jnp.exp(math.log(5.0) - 3.218876 * jax.random.uniform(arg_keys[4], (NX, NY), jnp.float32) ** steps_of(arg_keys[4], (NX, NY), ((0, 16),), -0.2, 0.2)), 0.2, 5.0)
    survey = jnp.clip(0.2 + 1.8 * jax.random.uniform(part_splits[5], (2, NX, NY), jnp.float32) ** steps_of(part_splits[5], (2, NX, NY), ((1, 16),), -0.2, 0.2), 0.2, 2.0)
    return dict(season_ids=season_ids, season_table=season_table, shelf_mask=shelf_mask, codes=codes, spawn=spawn, survey=survey)


RELAXATION = 0.8
MORTALITY_SCALE = 0.03
DRIFT_SCALE = 0.5


def neighbours(field):
    padded = jnp.pad(field, ((0, 0), (1, 1), (1, 1)))
    return padded[:, :-2, 1:-1], padded[:, 2:, 1:-1], padded[:, 1:-1, :-2], padded[:, 1:-1, 2:]


def restrict(field):
    return field.reshape(field.shape[0], field.shape[1] // 2, 2, field.shape[2] // 2, 2).sum(axis=(2, 4))


def prolong(field):
    return jnp.repeat(jnp.repeat(field, 2, axis=1), 2, axis=2)


def relax(iterate, forcing, operator, shelf, diagonal):
    return iterate + RELAXATION * shelf * (forcing - operator(iterate)) / diagonal


def jacobi_sweeps(forcing, shelf, diagonal, operator):
    iterate = RELAXATION * shelf * forcing / diagonal
    for repeat_index in range(COARSE_SWEEPS - 1):
        iterate = relax(iterate, forcing, operator, shelf, diagonal)
    return iterate


def diffusion_operator(diagonal, diffusion):
    def operate(field):
        before_x, after_x, before_y, after_y = neighbours(field)
        return diagonal * field - diffusion * (before_x + after_x + before_y + after_y)
    return operate


def forward_operator(diagonal, diffusion, drift_x, drift_y, westward, southward):
    def operate(field):
        before_x, after_x, before_y, after_y = neighbours(field)
        beside = before_x + after_x + before_y + after_y
        upwind_x = jnp.where(westward, before_x, after_x)
        upwind_y = jnp.where(southward, before_y, after_y)
        return diagonal * field - diffusion * beside - drift_x * upwind_x - drift_y * upwind_y
    return operate


def adjoint_operator(diagonal, diffusion, drift_x, drift_y, westward, southward):
    def operate(field):
        before_x, after_x, before_y, after_y = neighbours(field)
        beside = before_x + after_x + before_y + after_y
        taken_x = neighbours(jnp.where(westward, field, 0.0))[1] + neighbours(jnp.where(westward, 0.0, field))[0]
        taken_y = neighbours(jnp.where(southward, field, 0.0))[3] + neighbours(jnp.where(southward, 0.0, field))[2]
        return diagonal * field - diffusion * beside - drift_x * taken_x - drift_y * taken_y
    return operate


def vcycle(level_index, forcing, iterate, operators, shelves, diagonals, coarse_solve):
    shelf = shelves[level_index]
    diagonal = diagonals[level_index]
    if level_index == LEVELS:
        return coarse_solve(forcing, shelf, diagonal)
    operator = operators[level_index]
    if iterate is None:
        iterate = RELAXATION * shelf * forcing / diagonal
    else:
        iterate = relax(iterate, forcing, operator, shelf, diagonal)
    residual = shelf * (forcing - operator(iterate))
    correction = vcycle(level_index + 1, restrict(residual), None, operators, shelves, diagonals, coarse_solve)
    iterate = iterate + shelf * prolong(correction)
    return relax(iterate, forcing, operator, shelf, diagonal)


def reference(season_ids, season_table, shelf_mask, codes, spawn, survey):
    picked = season_table[:, season_ids]
    mortality = (MORTALITY_SCALE * picked[0])[:, None, None]
    diffusion = picked[1][:, None, None]
    drift_x = (DRIFT_SCALE * picked[2])[:, None, None]
    drift_y = (DRIFT_SCALE * picked[3])[:, None, None]
    spawn_scale = picked[4][:, None, None]
    shelves = [jnp.where(shelf_mask > 0, 1.0, 0.0).astype(jnp.float32)[None]]
    for level_index in range(LEVELS):
        shelves.append(jnp.where(restrict(shelves[-1]) > 0.0, 1.0, 0.0).astype(jnp.float32))
    westward = (codes % 2 == 0)[None]
    southward = (codes // 2 == 0)[None]
    diagonals = [mortality + 4.0 * diffusion + drift_x + drift_y]
    coarse_ops = []
    for level_index in range(1, LEVELS + 1):
        level_diffusion = diffusion * (2.0 ** level_index)
        level_diagonal = mortality * (4.0 ** level_index) + 4.0 * level_diffusion
        diagonals.append(level_diagonal)
        coarse_ops.append(diffusion_operator(level_diagonal, level_diffusion))
    forward_ops = [forward_operator(diagonals[0], diffusion, drift_x, drift_y, westward, southward)] + coarse_ops
    adjoint_ops = [adjoint_operator(diagonals[0], diffusion, drift_x, drift_y, westward, southward)] + coarse_ops

    def coarse_solve(forcing, shelf, diagonal):
        return jacobi_sweeps(forcing, shelf, diagonal, coarse_ops[-1])

    source = shelves[0] * spawn_scale * spawn[None]
    concentration = None
    for cycle_index in range(CYCLES):
        concentration = vcycle(0, source, concentration, forward_ops, shelves, diagonals, coarse_solve)
    misfit = jnp.mean(concentration, axis=0) - survey[0]
    target = jnp.broadcast_to(shelves[0] * (survey[1] * misfit / SEASONS)[None], concentration.shape)
    adjoint = None
    for cycle_index in range(CYCLES):
        adjoint = vcycle(0, target, adjoint, adjoint_ops, shelves, diagonals, coarse_solve)
    gradient = shelves[0][0] * jnp.sum(spawn_scale * adjoint, axis=0)
    return concentration, adjoint, gradient
```

```python
import functools

import jax
import jax.numpy as jnp
from jax import lax
from jax.experimental import pallas as pl
from jax.experimental.pallas import tpu as pltpu
from jax.sharding import PartitionSpec as P


f32, bf16 = jnp.float32, jnp.bfloat16
REACH = 8
STRIP = 8
HALO = 6


def wide(p, width):
    return jnp.concatenate([p] * (width // 128), axis=1) if width > 128 else p


def kernel(n, ny, prm, mask, codes, spawn, survey, c_out, a_out, g_out,
           strips, tgt, s0, west, south, f0, cn, cs, cw, ce, f1, it, up, dl,
           s1, k1, b1, u1, v1, s2, k2, b2, u2, s3own, b3own, win,
           send_n, recv_n, send_g, recv_g):
    me = lax.axis_index("tile")
    n1, n2, n3 = ny // 2, ny // 4, ny // 8

    def guarded(d, body):
        ok = (me + d >= 0) & (me + d < n)
        pl.when(ok)(body)

    strips[...] = jnp.zeros_like(strips)
    tgt[...] = jnp.zeros_like(tgt)
    f1[...] = jnp.zeros_like(f1)
    b2[...] = jnp.zeros_like(b2)
    win[...] = jnp.zeros_like(win)
    strips[0, STRIP:2 * STRIP, :] = jnp.where(mask[...] > 0, 1.0, 0.0).astype(f32)
    strips[1, STRIP:2 * STRIP, :] = codes[...].astype(f32)
    strips[2, STRIP:2 * STRIP, :] = spawn[...]
    barrier = pltpu.get_barrier_semaphore()
    offsets = [d for k in range(1, REACH + 1) for d in (-k, k)]
    for d in offsets:
        guarded(d, lambda d=d: pl.semaphore_signal(
            barrier, inc=1, device_id={"tile": me + d}, device_id_type=pl.DeviceIdType.MESH))
    pl.semaphore_wait(barrier, jnp.minimum(me, REACH) + jnp.minimum(n - 1 - me, REACH))

    def copy(src, dst, ssem, rsem, d):
        return pltpu.make_async_remote_copy(
            src_ref=src, dst_ref=dst, send_sem=ssem, recv_sem=rsem,
            device_id={"tile": me + d}, device_id_type=pl.DeviceIdType.MESH)

    def swap(k, up_src, up_dst, down_src, down_dst):
        def at(d):
            side = 0 if d < 0 else 1
            src, dst = (up_src, up_dst) if d < 0 else (down_src, down_dst)
            return copy(src, dst, send_n.at[k, side], recv_n.at[k, side], d)
        for d in (-1, 1):
            guarded(d, lambda d=d: at(d).start())
        guarded(1, lambda: copy(up_src, up_dst, send_n.at[k, 0], recv_n.at[k, 0], 1).wait_recv())
        guarded(-1, lambda: copy(down_src, down_dst, send_n.at[k, 1], recv_n.at[k, 1], -1).wait_recv())
        for d in (-1, 1):
            guarded(d, lambda d=d: at(d).wait_send())

    def gather_start(k, src):
        for d in offsets:
            guarded(d, lambda d=d: copy(src, win.at[k, REACH - d], send_g.at[k, REACH - d],
                                        recv_g.at[k, REACH - d], d).start())

    def gather_wait(k, src):
        for d in offsets:
            guarded(d, lambda d=d: copy(src, win.at[k, REACH + d], send_g.at[k, REACH + d],
                                        recv_g.at[k, REACH + d], d).wait_recv())
        for d in offsets:
            guarded(d, lambda d=d: copy(src, win.at[k, REACH - d], send_g.at[k, REACH - d],
                                        recv_g.at[k, REACH - d], d).wait_send())

    swap(0, strips.at[:, 8:16], strips.at[:, 16:24], strips.at[:, 8:16], strips.at[:, 0:8])

    gi = lax.broadcasted_iota(jnp.int32, (256, 128), 0)
    gj = lax.broadcasted_iota(jnp.int32, (256, 128), 1)
    pair_sum = jnp.where(gi // 2 == gj, 1.0, 0.0).astype(bf16)
    hi_ = lax.broadcasted_iota(jnp.int32, (128, 256), 0)
    hj_ = lax.broadcasted_iota(jnp.int32, (128, 256), 1)
    spread = jnp.where(hj_ // 2 == hi_, 1.0, 0.0).astype(bf16)

    def times(x, m):
        big = x.astype(bf16)
        rest = (x - big.astype(f32)).astype(bf16)
        return (jnp.dot(big, m, preferred_element_type=f32)
                + jnp.dot(rest, m, preferred_element_type=f32))

    def restrict(src, lo, count, width):
        blocks = width // 256
        stack = []
        for i in range(count):
            x = src[lo + 2 * i] + src[lo + 2 * i + 1]
            stack += [x[:, b * 256:(b + 1) * 256] for b in range(blocks)]
        y = times(jnp.concatenate(stack, axis=0), pair_sum)
        rows = []
        for i in range(count):
            parts = [y[(i * blocks + b) * 8:(i * blocks + b + 1) * 8] for b in range(blocks)]
            rows.append(jnp.concatenate(parts, axis=1) if blocks > 1 else parts[0])
        return rows

    def prolong(rows):
        blocks = rows[0].shape[1] // 128
        stack = [x[:, b * 128:(b + 1) * 128] for x in rows for b in range(blocks)]
        y = times(jnp.concatenate(stack, axis=0), spread)
        out = []
        for i in range(len(rows)):
            parts = [y[(i * blocks + b) * 8:(i * blocks + b + 1) * 8] for b in range(blocks)]
            out.append(jnp.concatenate(parts, axis=1) if blocks > 1 else parts[0])
        return out

    def lanes(width):
        return lax.broadcasted_iota(jnp.int32, (8, width), 1)

    def shifted(x):
        width = x.shape[1]
        lane = lanes(width)
        return (jnp.where(lane == 0, 0.0, pltpu.roll(x, 1, 1)),
                jnp.where(lane == width - 1, 0.0, pltpu.roll(x, width - 1, 1)))

    g0, dd, uu, vv, strength = prm[0], prm[1], prm[2], prm[3], prm[4]
    kappa = [None, prm[5], prm[6], prm[7]]
    ratio = [prm[8], prm[9], prm[10]]

    for r in range(24):
        s0[r] = jnp.broadcast_to(strips[0, r:r + 1, :], (8, ny))
        code = strips[1, r:r + 1, :]
        top = jnp.where(code >= 2.0, 1.0, 0.0)
        west[r] = jnp.broadcast_to(1.0 - (code - 2.0 * top), (8, ny))
        south[r] = jnp.broadcast_to(1.0 - top, (8, ny))
        f0[r] = s0[r] * wide(g0 * strength, ny) * jnp.broadcast_to(strips[2, r:r + 1, :], (8, ny))
    for i, x in enumerate(restrict(s0, 0, 12, ny)):
        s1[i] = jnp.where(x > 0.0, 1.0, 0.0)
        k1[i] = s1[i] * wide(kappa[1], n1)
    for i, x in enumerate(restrict(s1, 0, 6, n1)):
        s2[i] = jnp.where(x > 0.0, 1.0, 0.0)
        k2[i] = s2[i] * wide(kappa[2], n2)
    own3 = restrict(s2, 2, 1, n2)[0]
    s3own[...] = jnp.where(own3 > 0.0, 1.0, 0.0)
    gather_start(0, s3own)

    def loop(lo, hi, body):
        lax.fori_loop(lo, hi, lambda r, c: (body(r), c)[1], 0)

    def coefficients(adjoint):
        D = wide(dd, ny)
        U = wide(uu, ny)
        V = wide(vv, ny)

        def row(r):
            lane = lanes(ny)
            s = s0[r]
            if adjoint:
                an, as_ = 1.0 - west[r - 1], west[r + 1]
                so = south[r]
                bw, be = 1.0 - pltpu.roll(so, 1, 1), pltpu.roll(so, ny - 1, 1)
            else:
                an, bw = west[r], south[r]
                as_, be = 1.0 - an, 1.0 - bw
            cn[r] = s * (D + U * an)
            cs[r] = s * (D + U * as_)
            cw[r] = jnp.where(lane == 0, 0.0, s * (D + V * bw))
            ce[r] = jnp.where(lane == ny - 1, 0.0, s * (D + V * be))
        loop(3, 21, row)

    def relaxed0(f, r):
        x = f[r]
        return (0.2 * x + f0[r] + (cn[r] * f[r - 1] + cs[r] * f[r + 1])
                + (cw[r] * pltpu.roll(x, 1, 1) + ce[r] * pltpu.roll(x, ny - 1, 1)))

    def relaxed(f, b, k, r):
        x = f[r]
        w, e = shifted(x)
        return 0.2 * x + b[r] + k[r] * ((f[r - 1] + f[r + 1]) + (w + e))

    def coarse(k, s3):
        src = win[k]
        b = jnp.concatenate([src[i] for i in range(2 * REACH + 1)], axis=0)
        weight = jnp.concatenate([s3[i] * kappa[3] for i in range(2 * REACH + 1)], axis=0)
        lane = lax.broadcasted_iota(jnp.int32, b.shape, 1)
        left = jnp.where(lane == 0, 0.0, weight)
        right = jnp.where(lane == n3 - 1, 0.0, weight)
        zero = jnp.zeros((8, n3), f32)
        x = b
        for _ in range(7):
            above = jnp.concatenate([zero, x[:-8]], axis=0)
            below = jnp.concatenate([x[8:], zero], axis=0)
            x = (0.2 * x + b + weight * (above + below)
                 + (left * pltpu.roll(x, 1, 1) + right * pltpu.roll(x, n3 - 1, 1)))
        mid = REACH * 8
        return [x[mid - 8:mid], x[mid:mid + 8], x[mid + 8:mid + 16]]

    def below(f, turn, first_gather):
        def change(r):
            dl[r] = relaxed0(f, r) - f[r]
        loop(4, 20, change)
        for i, x in enumerate(restrict(dl, 4, 8, ny)):
            b1[2 + i] = x * wide(ratio[0], n1) * s1[2 + i]
        for r in range(4, 8):
            u1[r] = relaxed(b1, b1, k1, r) - b1[r]
        bb = b2.at[turn]
        for i, x in enumerate(restrict(u1, 4, 2, n1)):
            bb[2 + i] = x * wide(ratio[1], n2) * s2[2 + i]
        swap(4 + turn, bb.at[2:4], bb.at[4:6], bb.at[2:4], bb.at[0:2])
        for r in range(2, 4):
            u2[r] = relaxed(bb, bb, k2, r) - bb[r]
        mine = restrict(u2, 2, 1, n2)[0] * ratio[2] * s3own[...]
        own = b3own.at[turn]
        own[...] = mine
        win[1 + turn, REACH] = mine
        gather_start(1 + turn, own)
        if first_gather:
            win[0, REACH] = s3own[...]
            gather_wait(0, s3own)
        gather_wait(1 + turn, own)
        f3 = coarse(1 + turn, win[0])
        for i, x in enumerate(prolong(f3)):
            for j in (0, 1):
                r = 2 * i + j
                u2[r] = bb[r] + s2[r] * x
        f2 = [relaxed(u2, bb, k2, r) for r in range(1, 5)]
        for i, x in enumerate(prolong(f2)):
            for j in (0, 1):
                r = 2 + 2 * i + j
                u1[r] = b1[r] + s1[r] * x
        for r in range(3, 9):
            v1[r] = relaxed(u1, b1, k1, r)
        for i, x in enumerate(prolong([v1[r] for r in range(3, 9)])):
            for j in (0, 1):
                r = 6 + 2 * i + j
                up[r] = f[r] + s0[r] * x

    def solve(which, out, finish):
        turn = 2 * which
        below(f0, turn, which == 0)
        second = f1.at[which]

        def first(r):
            second[r] = relaxed0(up, r)
        loop(8, 16, first)
        swap(1 + which, second.at[8:8 + HALO], second.at[16:16 + HALO],
             second.at[16 - HALO:16], second.at[8 - HALO:8])

        def again(r):
            it[r] = relaxed0(second, r)
        loop(3, 21, again)
        below(it, turn + 1, False)
        for r in range(8):
            x = relaxed0(up, r + 8)
            out[r] = x
            finish(r, x)

    def to_target(r, x):
        misfit = jnp.sum(x, axis=0, keepdims=True) / 8.0 - survey[0, r:r + 1, :]
        tgt[8 + r:9 + r, :] = survey[1, r:r + 1, :] * misfit / 8.0

    def to_gradient(r, x):
        g_out[r:r + 1, :] = strips[0, 8 + r:9 + r, :] * jnp.sum(
            wide(strength, ny) * x, axis=0, keepdims=True)

    coefficients(False)
    solve(0, c_out, to_target)
    swap(3, tgt.at[8:16], tgt.at[16:24], tgt.at[8:16], tgt.at[0:8])
    for r in range(24):
        f0[r] = s0[r] * wide(g0, ny) * jnp.broadcast_to(tgt[r:r + 1, :], (8, ny))
    coefficients(True)
    solve(1, a_out, to_gradient)


def on_device(n, season_ids, season_table, shelf_mask, codes, spawn, survey):
    onehot = season_ids[:, None] == jnp.arange(season_table.shape[1], dtype=jnp.int32)[None, :]
    picked = jnp.sum(jnp.where(onehot[None], season_table[:, None, :], 0.0), axis=2)
    m, d, u, v, a = 0.03 * picked[0], picked[1], 0.5 * picked[2], 0.5 * picked[3], picked[4]
    diag = [m + 4.0 * d + u + v] + [4.0 ** l * m + 4.0 * 2.0 ** l * d for l in (1, 2, 3)]
    w = [0.8 / x for x in diag]
    prm = jnp.stack([w[0], w[0] * d, w[0] * u, w[0] * v, a,
                     w[1] * 2.0 * d, w[2] * 4.0 * d, w[3] * 8.0 * d,
                     diag[0] / diag[1], diag[1] / diag[2], diag[2] / diag[3]])
    prm = jnp.broadcast_to(prm[:, :, None], prm.shape + (128,))
    rows, ny = shelf_mask.shape
    fine = pltpu.VMEM((24, 8, ny), f32)
    lvl1 = pltpu.VMEM((12, 8, ny // 2), f32)
    lvl2 = pltpu.VMEM((6, 8, ny // 4), f32)
    slots = 2 * REACH + 1
    vm = pl.BlockSpec(memory_space=pltpu.VMEM)
    c, adj, g = pl.pallas_call(
        functools.partial(kernel, n, ny),
        out_shape=(jax.ShapeDtypeStruct((rows, 8, ny), f32),
                   jax.ShapeDtypeStruct((rows, 8, ny), f32),
                   jax.ShapeDtypeStruct((rows, ny), f32)),
        in_specs=[vm] * 5,
        out_specs=(vm, vm, vm),
        scratch_shapes=[
            pltpu.VMEM((3, 24, ny), f32), pltpu.VMEM((24, ny), f32),
            fine, fine, fine, fine, fine, fine, fine, fine,
            pltpu.VMEM((2, 24, 8, ny), f32), fine, fine, fine,
            lvl1, lvl1, lvl1, lvl1, lvl1, lvl2, lvl2,
            pltpu.VMEM((4, 6, 8, ny // 4), f32), lvl2,
            pltpu.VMEM((8, ny // 8), f32), pltpu.VMEM((4, 8, ny // 8), f32),
            pltpu.VMEM((5, slots, 8, ny // 8), f32),
            pltpu.SemaphoreType.DMA((8, 2)), pltpu.SemaphoreType.DMA((8, 2)),
            pltpu.SemaphoreType.DMA((5, slots)), pltpu.SemaphoreType.DMA((5, slots)),
        ],
        compiler_params=pltpu.CompilerParams(
            collective_id=0, has_side_effects=True, vmem_limit_bytes=48 << 20),
        cost_estimate=pl.CostEstimate(flops=60_000_000, bytes_accessed=1_000_000, transcendentals=0),
    )(prm, shelf_mask, codes, spawn, survey)
    return jnp.transpose(c, (1, 0, 2)), jnp.transpose(adj, (1, 0, 2)), g


def solution(mesh):
    in_specs = (P("peel"), P(), P("tile", None), P("tile", None), P("tile", None),
                P("peel", "tile", None))
    out_specs = (P("peel", "tile", None), P("peel", "tile", None), P("tile", "peel"))
    return jax.shard_map(
        functools.partial(on_device, mesh.shape["tile"]), mesh=mesh,
        in_specs=in_specs, out_specs=out_specs, check_vma=False)
```

```python
import functools

import jax
import jax.numpy as jnp
from jax import lax
from jax.experimental import pallas as pl
from jax.experimental.pallas import tpu as pltpu
from jax.sharding import PartitionSpec as P


f32, bf16 = jnp.float32, jnp.bfloat16
REACH = 8
STRIP = 8
HALO = 5


def wide(p, width):
    return jnp.concatenate([p] * (width // 128), axis=1) if width > 128 else p


def kernel(n, ny, ids, table, mask, codes, spawn, survey, c_out, a_out, g_out,
           strips, tgt, s0, west, south, f0, cn, cs, cw, ce, f1, it, up, dl,
           s1, k1, b1, u1, v1, s2, k2, b2, u2, s3own, b3own, win,
           send_n, recv_n, send_g, recv_g):
    me = lax.axis_index("tile")
    n1, n2, n3 = ny // 2, ny // 4, ny // 8

    def guarded(d, body):
        ok = (me + d >= 0) & (me + d < n)
        pl.when(ok)(body)

    strips[...] = jnp.zeros_like(strips)
    tgt[...] = jnp.zeros_like(tgt)
    f1[...] = jnp.zeros_like(f1)
    b2[...] = jnp.zeros_like(b2)
    win[...] = jnp.zeros_like(win)
    strips[0, STRIP:2 * STRIP, :] = jnp.where(mask[...] > 0, 1.0, 0.0).astype(f32)
    strips[1, STRIP:2 * STRIP, :] = codes[...].astype(f32)
    strips[2, STRIP:2 * STRIP, :] = spawn[...]
    barrier = pltpu.get_barrier_semaphore()
    offsets = [d for k in range(1, REACH + 1) for d in (-k, k)]
    for d in offsets:
        guarded(d, lambda d=d: pl.semaphore_signal(
            barrier, inc=1, device_id={"tile": me + d}, device_id_type=pl.DeviceIdType.MESH))
    pl.semaphore_wait(barrier, jnp.minimum(me, REACH) + jnp.minimum(n - 1 - me, REACH))

    def copy(src, dst, ssem, rsem, d):
        return pltpu.make_async_remote_copy(
            src_ref=src, dst_ref=dst, send_sem=ssem, recv_sem=rsem,
            device_id={"tile": me + d}, device_id_type=pl.DeviceIdType.MESH)

    pending = []

    def swap(k, up_src, up_dst, down_src, down_dst):
        def at(d):
            side = 0 if d < 0 else 1
            src, dst = (up_src, up_dst) if d < 0 else (down_src, down_dst)
            return copy(src, dst, send_n.at[k, side], recv_n.at[k, side], d)
        for d in (-1, 1):
            guarded(d, lambda d=d: at(d).start())
            pending.append((d, lambda d=d: at(d).wait_send()))

    def arrive(k, up_src, up_dst, down_src, down_dst):
        guarded(1, lambda: copy(up_src, up_dst, send_n.at[k, 0], recv_n.at[k, 0], 1).wait_recv())
        guarded(-1, lambda: copy(down_src, down_dst, send_n.at[k, 1], recv_n.at[k, 1], -1).wait_recv())

    def gather_start(k, src):
        for d in offsets:
            guarded(d, lambda d=d: copy(src, win.at[k, REACH - d], send_g.at[k, REACH - d],
                                        recv_g.at[k, REACH - d], d).start())
            pending.append((d, lambda d=d: copy(
                src, win.at[k, REACH - d], send_g.at[k, REACH - d],
                recv_g.at[k, REACH - d], d).wait_send()))

    def gather_wait(k, src):
        for d in offsets:
            guarded(d, lambda d=d: copy(src, win.at[k, REACH + d], send_g.at[k, REACH + d],
                                        recv_g.at[k, REACH + d], d).wait_recv())

    ends = (strips.at[:, 8:16], strips.at[:, 16:24], strips.at[:, 8:16], strips.at[:, 0:8])
    swap(0, *ends)
    arrive(0, *ends)

    gi = lax.broadcasted_iota(jnp.int32, (256, 128), 0)
    gj = lax.broadcasted_iota(jnp.int32, (256, 128), 1)
    pair_sum = jnp.where(gi // 2 == gj, 1.0, 0.0).astype(bf16)
    hi_ = lax.broadcasted_iota(jnp.int32, (128, 256), 0)
    hj_ = lax.broadcasted_iota(jnp.int32, (128, 256), 1)
    spread = jnp.where(hj_ // 2 == hi_, 1.0, 0.0).astype(bf16)

    def times(x, m):
        big = x.astype(bf16)
        rest = (x - big.astype(f32)).astype(bf16)
        return (jnp.dot(big, m, preferred_element_type=f32)
                + jnp.dot(rest, m, preferred_element_type=f32))

    def restrict(src, lo, count, width):
        blocks = width // 256
        stack = []
        for i in range(count):
            x = src[lo + 2 * i] + src[lo + 2 * i + 1]
            stack += [x[:, b * 256:(b + 1) * 256] for b in range(blocks)]
        y = times(jnp.concatenate(stack, axis=0), pair_sum)
        rows = []
        for i in range(count):
            parts = [y[(i * blocks + b) * 8:(i * blocks + b + 1) * 8] for b in range(blocks)]
            rows.append(jnp.concatenate(parts, axis=1) if blocks > 1 else parts[0])
        return rows

    def prolong(rows):
        blocks = rows[0].shape[1] // 128
        stack = [x[:, b * 128:(b + 1) * 128] for x in rows for b in range(blocks)]
        y = times(jnp.concatenate(stack, axis=0), spread)
        out = []
        for i in range(len(rows)):
            parts = [y[(i * blocks + b) * 8:(i * blocks + b + 1) * 8] for b in range(blocks)]
            out.append(jnp.concatenate(parts, axis=1) if blocks > 1 else parts[0])
        return out

    def lanes(width):
        return lax.broadcasted_iota(jnp.int32, (8, width), 1)

    def shifted(x):
        width = x.shape[1]
        lane = lanes(width)
        return (jnp.where(lane == 0, 0.0, pltpu.roll(x, 1, 1)),
                jnp.where(lane == width - 1, 0.0, pltpu.roll(x, width - 1, 1)))

    one = ids[...] == lax.broadcasted_iota(jnp.int32, (8, table.shape[1]), 1)

    def pick(k):
        x = jnp.sum(jnp.where(one, table[k:k + 1, :], 0.0), axis=1, keepdims=True)
        return jnp.broadcast_to(x, (8, 128))
    mort, diff, strength = 0.03 * pick(0), pick(1), pick(4)
    u, v = 0.5 * pick(2), 0.5 * pick(3)
    diag = [mort + 4.0 * diff + u + v]
    diag += [4.0 ** l * mort + 4.0 * 2.0 ** l * diff for l in (1, 2, 3)]
    w = [0.8 / x for x in diag]
    g0, dd, uu, vv = w[0], w[0] * diff, w[0] * u, w[0] * v
    kappa = [2.0 ** l * diff * w[l] for l in range(4)]
    ratio = [diag[l] / diag[l + 1] for l in range(3)]

    for r in range(24):
        s0[r] = jnp.broadcast_to(strips[0, r:r + 1, :], (8, ny))
        code = strips[1, r:r + 1, :]
        top = jnp.where(code >= 2.0, 1.0, 0.0)
        west[r] = jnp.broadcast_to(1.0 - (code - 2.0 * top), (8, ny))
        south[r] = jnp.broadcast_to(1.0 - top, (8, ny))
        f0[r] = s0[r] * wide(g0 * strength, ny) * jnp.broadcast_to(strips[2, r:r + 1, :], (8, ny))
    for i, x in enumerate(restrict(s0, 0, 12, ny)):
        s1[i] = jnp.where(x > 0.0, 1.0, 0.0)
        k1[i] = s1[i] * wide(kappa[1], n1)
    for i, x in enumerate(restrict(s1, 0, 6, n1)):
        s2[i] = jnp.where(x > 0.0, 1.0, 0.0)
        k2[i] = s2[i] * wide(kappa[2], n2)
    own3 = restrict(s2, 2, 1, n2)[0]
    s3own[...] = jnp.where(own3 > 0.0, 1.0, 0.0)
    gather_start(0, s3own)

    def loop(lo, hi, body):
        lax.fori_loop(lo, hi, lambda r, c: (body(r), c)[1], 0)

    def coefficients(adjoint):
        D = wide(dd, ny)
        U = wide(uu, ny)
        V = wide(vv, ny)

        def row(r):
            lane = lanes(ny)
            s = s0[r]
            if adjoint:
                an, as_ = 1.0 - west[r - 1], west[r + 1]
                so = south[r]
                bw, be = 1.0 - pltpu.roll(so, 1, 1), pltpu.roll(so, ny - 1, 1)
            else:
                an, bw = west[r], south[r]
                as_, be = 1.0 - an, 1.0 - bw
            cn[r] = s * (D + U * an)
            cs[r] = s * (D + U * as_)
            cw[r] = jnp.where(lane == 0, 0.0, s * (D + V * bw))
            ce[r] = jnp.where(lane == ny - 1, 0.0, s * (D + V * be))
        loop(3, 21, row)

    def relaxed0(f, r):
        x = f[r]
        return (0.2 * x + f0[r] + (cn[r] * f[r - 1] + cs[r] * f[r + 1])
                + (cw[r] * pltpu.roll(x, 1, 1) + ce[r] * pltpu.roll(x, ny - 1, 1)))

    def relaxed(f, b, k, r):
        x = f[r]
        w, e = shifted(x)
        return 0.2 * x + b[r] + k[r] * ((f[r - 1] + f[r + 1]) + (w + e))

    def coarse(k, s3):
        src = win[k]
        b = jnp.concatenate([src[i] for i in range(2 * REACH + 1)], axis=0)
        weight = jnp.concatenate([s3[i] * kappa[3] for i in range(2 * REACH + 1)], axis=0)
        lane = lax.broadcasted_iota(jnp.int32, b.shape, 1)
        left = jnp.where(lane == 0, 0.0, weight)
        right = jnp.where(lane == n3 - 1, 0.0, weight)
        zero = jnp.zeros((8, n3), f32)
        x = b
        for _ in range(7):
            above = jnp.concatenate([zero, x[:-8]], axis=0)
            below = jnp.concatenate([x[8:], zero], axis=0)
            x = (0.2 * x + b + weight * (above + below)
                 + (left * pltpu.roll(x, 1, 1) + right * pltpu.roll(x, n3 - 1, 1)))
        mid = REACH * 8
        return [x[mid - 8:mid], x[mid:mid + 8], x[mid + 8:mid + 16]]

    def below(f, turn, first_gather):
        for i, x in enumerate(restrict(dl, 4, 8, ny)):
            b1[2 + i] = x * wide(ratio[0], n1) * s1[2 + i]
        for r in range(4, 8):
            u1[r] = relaxed(b1, b1, k1, r) - b1[r]
        bb = b2.at[turn]
        for i, x in enumerate(restrict(u1, 4, 2, n1)):
            bb[2 + i] = x * wide(ratio[1], n2) * s2[2 + i]
        ends = (bb.at[2:4], bb.at[4:6], bb.at[2:4], bb.at[0:2])
        swap(4 + turn, *ends)
        arrive(4 + turn, *ends)
        for r in range(2, 4):
            u2[r] = relaxed(bb, bb, k2, r) - bb[r]
        mine = restrict(u2, 2, 1, n2)[0] * ratio[2] * s3own[...]
        own = b3own.at[turn]
        own[...] = mine
        win[1 + turn, REACH] = mine
        gather_start(1 + turn, own)
        if first_gather:
            win[0, REACH] = s3own[...]
            gather_wait(0, s3own)
        gather_wait(1 + turn, own)
        f3 = coarse(1 + turn, win[0])
        for i, x in enumerate(prolong(f3)):
            for j in (0, 1):
                r = 2 * i + j
                u2[r] = bb[r] + s2[r] * x
        f2 = [relaxed(u2, bb, k2, r) for r in range(1, 5)]
        for i, x in enumerate(prolong(f2)):
            for j in (0, 1):
                r = 2 + 2 * i + j
                u1[r] = b1[r] + s1[r] * x
        for r in range(3, 9):
            v1[r] = relaxed(u1, b1, k1, r)
        for i, x in enumerate(prolong([v1[r] for r in range(3, 9)])):
            for j in (0, 1):
                r = 6 + 2 * i + j
                up[r] = f[r] + s0[r] * x

    def solve(which, out, finish):
        turn = 2 * which

        def change(f, lo, hi):
            def row(r):
                dl[r] = relaxed0(f, r) - f[r]
            loop(lo, hi, row)
        change(f0, 4, 20)
        below(f0, turn, which == 0)
        second = f1.at[which]

        def first(r):
            second[r] = relaxed0(up, r)
        loop(7, 17, first)
        ends = (second.at[9:9 + HALO], second.at[17:17 + HALO],
                second.at[15 - HALO:15], second.at[7 - HALO:7])
        swap(1 + which, *ends)

        def again(r):
            it[r] = relaxed0(second, r)
        loop(8, 16, again)
        change(it, 9, 15)
        arrive(1 + which, *ends)
        loop(3, 8, again)
        loop(16, 21, again)
        change(it, 4, 9)
        change(it, 15, 20)
        below(it, turn + 1, False)
        for r in range(8):
            x = relaxed0(up, r + 8)
            out[r] = x
            finish(r, x)

    def to_target(r, x):
        misfit = jnp.sum(x, axis=0, keepdims=True) / 8.0 - survey[0, r:r + 1, :]
        tgt[8 + r:9 + r, :] = survey[1, r:r + 1, :] * misfit / 8.0

    def to_gradient(r, x):
        g_out[r:r + 1, :] = strips[0, 8 + r:9 + r, :] * jnp.sum(
            wide(strength, ny) * x, axis=0, keepdims=True)

    coefficients(False)
    solve(0, c_out, to_target)
    ends = (tgt.at[8:16], tgt.at[16:24], tgt.at[8:16], tgt.at[0:8])
    swap(3, *ends)
    coefficients(True)
    arrive(3, *ends)
    for r in range(24):
        f0[r] = s0[r] * wide(g0, ny) * jnp.broadcast_to(tgt[r:r + 1, :], (8, ny))
    solve(1, a_out, to_gradient)
    for d, wait in pending:
        guarded(d, wait)


def on_device(n, season_ids, season_table, shelf_mask, codes, spawn, survey):
    rows, ny = shelf_mask.shape
    fine = pltpu.VMEM((24, 8, ny), f32)
    lvl1 = pltpu.VMEM((12, 8, ny // 2), f32)
    lvl2 = pltpu.VMEM((6, 8, ny // 4), f32)
    slots = 2 * REACH + 1
    vm = pl.BlockSpec(memory_space=pltpu.VMEM)
    c, adj, g = pl.pallas_call(
        functools.partial(kernel, n, ny),
        out_shape=(jax.ShapeDtypeStruct((rows, 8, ny), f32),
                   jax.ShapeDtypeStruct((rows, 8, ny), f32),
                   jax.ShapeDtypeStruct((rows, ny), f32)),
        in_specs=[vm] * 6,
        out_specs=(vm, vm, vm),
        scratch_shapes=[
            pltpu.VMEM((3, 24, ny), f32), pltpu.VMEM((24, ny), f32),
            fine, fine, fine, fine, fine, fine, fine, fine,
            pltpu.VMEM((2, 24, 8, ny), f32), fine, fine, fine,
            lvl1, lvl1, lvl1, lvl1, lvl1, lvl2, lvl2,
            pltpu.VMEM((4, 6, 8, ny // 4), f32), lvl2,
            pltpu.VMEM((8, ny // 8), f32), pltpu.VMEM((4, 8, ny // 8), f32),
            pltpu.VMEM((5, slots, 8, ny // 8), f32),
            pltpu.SemaphoreType.DMA((8, 2)), pltpu.SemaphoreType.DMA((8, 2)),
            pltpu.SemaphoreType.DMA((5, slots)), pltpu.SemaphoreType.DMA((5, slots)),
        ],
        compiler_params=pltpu.CompilerParams(
            collective_id=0, has_side_effects=True, vmem_limit_bytes=48 << 20),
        cost_estimate=pl.CostEstimate(flops=60_000_000, bytes_accessed=1_000_000, transcendentals=0),
    )(season_ids[:, None], season_table, shelf_mask, codes, spawn, survey)
    return jnp.transpose(c, (1, 0, 2)), jnp.transpose(adj, (1, 0, 2)), g


def solution(mesh):
    in_specs = (P("peel"), P(), P("tile", None), P("tile", None), P("tile", None),
                P("peel", "tile", None))
    out_specs = (P("peel", "tile", None), P("peel", "tile", None), P("tile", "peel"))
    return jax.shard_map(
        functools.partial(on_device, mesh.shape["tile"]), mesh=mesh,
        in_specs=in_specs, out_specs=out_specs, check_vma=False)
```

```python
import functools

import jax
import jax.numpy as jnp
from jax import lax
from jax.experimental import pallas as pl
from jax.experimental.pallas import tpu as pltpu
from jax.sharding import PartitionSpec as P


f32, bf16 = jnp.float32, jnp.bfloat16
REACH = 8
STRIP = 8
HALO = 5


def wide(p, width):
    return jnp.concatenate([p] * (width // 128), axis=1) if width > 128 else p


def kernel(n, ny, ids, table, mask_in, codes_in, spawn_in, survey_in, c_out, a_out, g_out,
           mask, codes, survey, load_sem, strips, tgt, s0, west, south, f0, cn, cs, cw, ce, f1, it, up, dl,
           s1, k1, b1, u1, v1, s2, k2, b2, u2, s3own, b3own, win,
           send_n, recv_n, send_g, recv_g):
    me = lax.axis_index("tile")
    n1, n2, n3 = ny // 2, ny // 4, ny // 8

    def guarded(d, body):
        ok = (me + d >= 0) & (me + d < n)
        pl.when(ok)(body)

    loads = [pltpu.make_async_copy(src, dst, load_sem.at[k]) for k, (src, dst) in enumerate(
        [(mask_in, mask), (codes_in, codes), (spawn_in, strips.at[2, 8:16]), (survey_in, survey)])]
    for load in loads:
        load.start()

    for lo in (0, 16):
        strips[:, lo:lo + 8, :] = jnp.zeros((3, 8, ny), f32)
    tgt[...] = jnp.zeros_like(tgt)
    for k in (0, 1):
        for lo in (0, 16):
            f1[k, lo:lo + 8] = jnp.zeros((8, 8, ny), f32)
    b2[...] = jnp.zeros_like(b2)
    win[...] = jnp.zeros_like(win)
    def loop(lo, hi, body):
        step = next(k for k in (4, 5, 3, 2, 1) if (hi - lo) % k == 0)

        def some(q, c):
            for k in range(step):
                body(lo + q * step + k)
            return c
        if hi - lo == step:
            some(0, 0)
        else:
            lax.fori_loop(0, (hi - lo) // step, some, 0)

    barrier = pltpu.get_barrier_semaphore()
    offsets = [d for k in range(1, REACH + 1) for d in (-k, k)]
    for d in offsets:
        guarded(d, lambda d=d: pl.semaphore_signal(
            barrier, inc=1, device_id={"tile": me + d}, device_id_type=pl.DeviceIdType.MESH))
    for load in loads[:3]:
        load.wait()
    strips[0, STRIP:2 * STRIP, :] = jnp.where(mask[...] > 0, 1.0, 0.0).astype(f32)
    strips[1, STRIP:2 * STRIP, :] = codes[...].astype(f32)

    def lanes(width):
        return lax.broadcasted_iota(jnp.int32, (8, width), 1)

    entries = lax.broadcasted_iota(jnp.int32, (8, table.shape[1]), 1)
    season = lax.broadcasted_iota(jnp.int32, (8, table.shape[1]), 0)
    wanted = jnp.full((8, table.shape[1]), ids[0], jnp.int32)
    for k in range(1, 8):
        wanted = jnp.where(season == k, ids[k], wanted)
    one = wanted == entries

    def pick(k):
        x = jnp.sum(jnp.where(one, table[k:k + 1, :], 0.0), axis=1, keepdims=True)
        return jnp.broadcast_to(x, (8, 128))
    mort, diff, strength = 0.03 * pick(0), pick(1), pick(4)
    u, v = 0.5 * pick(2), 0.5 * pick(3)
    diag = [mort + 4.0 * diff + u + v]
    diag += [4.0 ** l * mort + 4.0 * 2.0 ** l * diff for l in (1, 2, 3)]
    w = [0.8 / x for x in diag]
    g0, dd, uu, vv = w[0], w[0] * diff, w[0] * u, w[0] * v
    kappa = [2.0 ** l * diff * w[l] for l in range(4)]
    ratio = [diag[l] / diag[l + 1] for l in range(3)]

    def spread_row(r):
        s0[r] = jnp.broadcast_to(strips[0, r:r + 1, :], (8, ny))
        code = strips[1, r:r + 1, :]
        top = jnp.where(code >= 2.0, 1.0, 0.0)
        west[r] = jnp.broadcast_to(1.0 - (code - 2.0 * top), (8, ny))
        south[r] = jnp.broadcast_to(1.0 - top, (8, ny))
        f0[r] = s0[r] * wide(g0 * strength, ny) * jnp.broadcast_to(strips[2, r:r + 1, :], (8, ny))
    for r in range(8, 16):
        spread_row(r)

    def coefficients(adjoint, *ranges):
        D = wide(dd, ny)
        U = wide(uu, ny)
        V = wide(vv, ny)

        def row(r):
            lane = lanes(ny)
            s = s0[r]
            if adjoint:
                an, as_ = 1.0 - west[r - 1], west[r + 1]
                so = south[r]
                bw, be = 1.0 - pltpu.roll(so, 1, 1), pltpu.roll(so, ny - 1, 1)
            else:
                an, bw = west[r], south[r]
                as_, be = 1.0 - an, 1.0 - bw
            cn[r] = s * (D + U * an)
            cs[r] = s * (D + U * as_)
            cw[r] = jnp.where(lane == 0, 0.0, s * (D + V * bw))
            ce[r] = jnp.where(lane == ny - 1, 0.0, s * (D + V * be))
        for lo, hi in ranges:
            loop(lo, hi, row)

    pl.semaphore_wait(barrier, jnp.minimum(me, REACH) + jnp.minimum(n - 1 - me, REACH))

    def copy(src, dst, ssem, rsem, d):
        return pltpu.make_async_remote_copy(
            src_ref=src, dst_ref=dst, send_sem=ssem, recv_sem=rsem,
            device_id={"tile": me + d}, device_id_type=pl.DeviceIdType.MESH)

    pending = []

    def swap(k, up_src, up_dst, down_src, down_dst):
        def at(d):
            side = 0 if d < 0 else 1
            src, dst = (up_src, up_dst) if d < 0 else (down_src, down_dst)
            return copy(src, dst, send_n.at[k, side], recv_n.at[k, side], d)
        for d in (-1, 1):
            guarded(d, lambda d=d: at(d).start())
            pending.append((d, lambda d=d: at(d).wait_send()))

    def arrive(k, up_src, up_dst, down_src, down_dst):
        guarded(1, lambda: copy(up_src, up_dst, send_n.at[k, 0], recv_n.at[k, 0], 1).wait_recv())
        guarded(-1, lambda: copy(down_src, down_dst, send_n.at[k, 1], recv_n.at[k, 1], -1).wait_recv())

    def gather_start(k, src):
        for d in offsets[::-1]:
            guarded(d, lambda d=d: copy(src, win.at[k, REACH - d], send_g.at[k, REACH - d],
                                        recv_g.at[k, REACH - d], d).start())
            pending.append((d, lambda d=d: copy(
                src, win.at[k, REACH - d], send_g.at[k, REACH - d],
                recv_g.at[k, REACH - d], d).wait_send()))

    def gather_wait(k, src):
        for d in offsets:
            guarded(d, lambda d=d: copy(src, win.at[k, REACH + d], send_g.at[k, REACH + d],
                                        recv_g.at[k, REACH + d], d).wait_recv())

    ends = (strips.at[:, 8:16], strips.at[:, 16:24], strips.at[:, 8:16], strips.at[:, 0:8])
    swap(0, *ends)
    coefficients(False, (8, 16))
    arrive(0, *ends)
    for r in (*range(8), *range(16, 24)):
        spread_row(r)

    gi = lax.broadcasted_iota(jnp.int32, (256, 128), 0)
    gj = lax.broadcasted_iota(jnp.int32, (256, 128), 1)
    pair_sum = jnp.where(gi // 2 == gj, 1.0, 0.0).astype(bf16)
    hi_ = lax.broadcasted_iota(jnp.int32, (128, 256), 0)
    hj_ = lax.broadcasted_iota(jnp.int32, (128, 256), 1)
    spread = jnp.where(hj_ // 2 == hi_, 1.0, 0.0).astype(bf16)

    def times(x, m):
        big = x.astype(bf16)
        rest = (x - big.astype(f32)).astype(bf16)
        return (jnp.dot(big, m, preferred_element_type=f32)
                + jnp.dot(rest, m, preferred_element_type=f32))

    def restrict(src, lo, count, width):
        blocks = width // 256
        stack = []
        for i in range(count):
            x = src[lo + 2 * i] + src[lo + 2 * i + 1]
            stack += [x[:, b * 256:(b + 1) * 256] for b in range(blocks)]
        y = times(jnp.concatenate(stack, axis=0), pair_sum)
        rows = []
        for i in range(count):
            parts = [y[(i * blocks + b) * 8:(i * blocks + b + 1) * 8] for b in range(blocks)]
            rows.append(jnp.concatenate(parts, axis=1) if blocks > 1 else parts[0])
        return rows

    def prolong(rows):
        blocks = rows[0].shape[1] // 128
        stack = [x[:, b * 128:(b + 1) * 128] for x in rows for b in range(blocks)]
        y = times(jnp.concatenate(stack, axis=0), spread)
        out = []
        for i in range(len(rows)):
            parts = [y[(i * blocks + b) * 8:(i * blocks + b + 1) * 8] for b in range(blocks)]
            out.append(jnp.concatenate(parts, axis=1) if blocks > 1 else parts[0])
        return out

    def shifted(x):
        width = x.shape[1]
        lane = lanes(width)
        return (jnp.where(lane == 0, 0.0, pltpu.roll(x, 1, 1)),
                jnp.where(lane == width - 1, 0.0, pltpu.roll(x, width - 1, 1)))

    for i, x in enumerate(restrict(s0, 0, 12, ny)):
        s1[i] = jnp.where(x > 0.0, 1.0, 0.0)
        k1[i] = s1[i] * wide(kappa[1], n1)
    for i, x in enumerate(restrict(s1, 0, 6, n1)):
        s2[i] = jnp.where(x > 0.0, 1.0, 0.0)
        k2[i] = s2[i] * wide(kappa[2], n2)
    own3 = restrict(s2, 2, 1, n2)[0]
    s3own[...] = jnp.where(own3 > 0.0, 1.0, 0.0)
    gather_start(0, s3own)

    def relaxed0(f, r):
        x = f[r]
        return (0.2 * x + f0[r] + (cn[r] * f[r - 1] + cs[r] * f[r + 1])
                + (cw[r] * pltpu.roll(x, 1, 1) + ce[r] * pltpu.roll(x, ny - 1, 1)))

    def relaxed(f, b, k, r):
        x = f[r]
        w, e = shifted(x)
        return 0.2 * x + b[r] + k[r] * ((f[r - 1] + f[r + 1]) + (w + e))

    def coarse(k, s3):
        src = win[k]
        b = jnp.concatenate([src[i] for i in range(2 * REACH + 1)], axis=0)
        weight = jnp.concatenate([s3[i] * kappa[3] for i in range(2 * REACH + 1)], axis=0)
        lane = lax.broadcasted_iota(jnp.int32, b.shape, 1)
        left = jnp.where(lane == 0, 0.0, weight)
        right = jnp.where(lane == n3 - 1, 0.0, weight)
        zero = jnp.zeros((8, n3), f32)
        x = b
        for _ in range(7):
            above = jnp.concatenate([zero, x[:-8]], axis=0)
            below = jnp.concatenate([x[8:], zero], axis=0)
            x = (0.2 * x + b + weight * (above + below)
                 + (left * pltpu.roll(x, 1, 1) + right * pltpu.roll(x, n3 - 1, 1)))
        mid = REACH * 8
        return [x[mid - 8:mid], x[mid:mid + 8], x[mid + 8:mid + 16]]

    def below(f, turn, first_gather):
        for i, x in enumerate(restrict(dl, 4, 8, ny)):
            b1[2 + i] = x * wide(ratio[0], n1) * s1[2 + i]
        for r in range(4, 8):
            u1[r] = relaxed(b1, b1, k1, r) - b1[r]
        bb = b2.at[turn]
        for i, x in enumerate(restrict(u1, 4, 2, n1)):
            bb[2 + i] = x * wide(ratio[1], n2) * s2[2 + i]
        ends = (bb.at[2:4], bb.at[4:6], bb.at[2:4], bb.at[0:2])
        swap(4 + turn, *ends)
        arrive(4 + turn, *ends)
        for r in range(2, 4):
            u2[r] = relaxed(bb, bb, k2, r) - bb[r]
        mine = restrict(u2, 2, 1, n2)[0] * ratio[2] * s3own[...]
        own = b3own.at[turn]
        own[...] = mine
        win[1 + turn, REACH] = mine
        gather_start(1 + turn, own)
        if first_gather:
            win[0, REACH] = s3own[...]
            gather_wait(0, s3own)
        gather_wait(1 + turn, own)
        f3 = coarse(1 + turn, win[0])
        for i, x in enumerate(prolong(f3)):
            for j in (0, 1):
                r = 2 * i + j
                u2[r] = bb[r] + s2[r] * x
        f2 = [relaxed(u2, bb, k2, r) for r in range(1, 5)]
        for i, x in enumerate(prolong(f2)):
            for j in (0, 1):
                r = 2 + 2 * i + j
                u1[r] = b1[r] + s1[r] * x
        for r in range(3, 9):
            v1[r] = relaxed(u1, b1, k1, r)
        for i, x in enumerate(prolong([v1[r] for r in range(3, 9)])):
            for j in (0, 1):
                r = 6 + 2 * i + j
                up[r] = f[r] + s0[r] * x

    def solve(which, out, finish):
        turn = 2 * which

        def change(f, lo, hi):
            def row(r):
                dl[r] = relaxed0(f, r) - f[r]
            loop(lo, hi, row)
        change(f0, 4, 20)
        below(f0, turn, which == 0)
        second = f1.at[which]

        def first(r):
            second[r] = relaxed0(up, r)
        loop(7, 17, first)
        ends = (second.at[9:9 + HALO], second.at[17:17 + HALO],
                second.at[15 - HALO:15], second.at[7 - HALO:7])
        swap(1 + which, *ends)

        def again(r):
            it[r] = relaxed0(second, r)
        loop(8, 16, again)
        change(it, 9, 15)
        arrive(1 + which, *ends)
        loop(3, 8, again)
        loop(16, 21, again)
        change(it, 4, 9)
        change(it, 15, 20)
        below(it, turn + 1, False)
        for r in range(8):
            x = relaxed0(up, r + 8)
            out[r] = x
            finish(r, x)

    def to_target(r, x):
        misfit = jnp.sum(x, axis=0, keepdims=True) / 8.0 - survey[0, r:r + 1, :]
        tgt[8 + r:9 + r, :] = survey[1, r:r + 1, :] * misfit / 8.0

    def to_gradient(r, x):
        g_out[r:r + 1, :] = strips[0, 8 + r:9 + r, :] * jnp.sum(
            wide(strength, ny) * x, axis=0, keepdims=True)

    coefficients(False, (3, 8), (16, 21))
    loads[3].wait()
    solve(0, c_out, to_target)
    ends = (tgt.at[8:16], tgt.at[16:24], tgt.at[8:16], tgt.at[0:8])
    swap(3, *ends)
    coefficients(True, (3, 21))
    arrive(3, *ends)
    for r in range(24):
        f0[r] = s0[r] * wide(g0, ny) * jnp.broadcast_to(tgt[r:r + 1, :], (8, ny))
    solve(1, a_out, to_gradient)
    for d, wait in pending:
        guarded(d, wait)


def on_device(n, season_ids, season_table, shelf_mask, codes, spawn, survey):
    rows, ny = shelf_mask.shape
    fine = pltpu.VMEM((24, 8, ny), f32)
    lvl1 = pltpu.VMEM((12, 8, ny // 2), f32)
    lvl2 = pltpu.VMEM((6, 8, ny // 4), f32)
    slots = 2 * REACH + 1
    vm = pl.BlockSpec(memory_space=pltpu.VMEM)
    c, adj, g = pl.pallas_call(
        functools.partial(kernel, n, ny),
        out_shape=(jax.ShapeDtypeStruct((rows, 8, ny), f32),
                   jax.ShapeDtypeStruct((rows, 8, ny), f32),
                   jax.ShapeDtypeStruct((rows, ny), f32)),
        in_specs=[pl.BlockSpec(memory_space=pltpu.SMEM), vm] + [pl.BlockSpec(memory_space=pltpu.HBM)] * 4,
        out_specs=(vm, vm, vm),
        scratch_shapes=[
            pltpu.VMEM((rows, ny), jnp.int32), pltpu.VMEM((rows, ny), jnp.int32),
            pltpu.VMEM((2, rows, ny), f32), pltpu.SemaphoreType.DMA((4,)),
            pltpu.VMEM((3, 24, ny), f32), pltpu.VMEM((24, ny), f32),
            fine, fine, fine, fine, fine, fine, fine, fine,
            pltpu.VMEM((2, 24, 8, ny), f32), fine, fine, fine,
            lvl1, lvl1, lvl1, lvl1, lvl1, lvl2, lvl2,
            pltpu.VMEM((4, 6, 8, ny // 4), f32), lvl2,
            pltpu.VMEM((8, ny // 8), f32), pltpu.VMEM((4, 8, ny // 8), f32),
            pltpu.VMEM((5, slots, 8, ny // 8), f32),
            pltpu.SemaphoreType.DMA((8, 2)), pltpu.SemaphoreType.DMA((8, 2)),
            pltpu.SemaphoreType.DMA((5, slots)), pltpu.SemaphoreType.DMA((5, slots)),
        ],
        compiler_params=pltpu.CompilerParams(
            collective_id=0, has_side_effects=True, vmem_limit_bytes=48 << 20),
        cost_estimate=pl.CostEstimate(flops=60_000_000, bytes_accessed=1_000_000, transcendentals=0),
    )(season_ids, season_table, shelf_mask, codes, spawn, survey)
    return jnp.transpose(c, (1, 0, 2)), jnp.transpose(adj, (1, 0, 2)), g


def solution(mesh):
    in_specs = (P("peel"), P(), P("tile", None), P("tile", None), P("tile", None),
                P("peel", "tile", None))
    out_specs = (P("peel", "tile", None), P("peel", "tile", None), P("tile", "peel"))
    return jax.shard_map(
        functools.partial(on_device, mesh.shape["tile"]), mesh=mesh,
        in_specs=in_specs, out_specs=out_specs, check_vma=False)
```

```python
import functools

import jax
import jax.numpy as jnp
from jax import lax
from jax.experimental import pallas as pl
from jax.experimental.pallas import tpu as pltpu
from jax.sharding import PartitionSpec as P


f32, bf16 = jnp.float32, jnp.bfloat16
REACH = 9
STRIP = 8
HALO = 5


def wide(p, width):
    return jnp.concatenate([p] * (width // 128), axis=1) if width > 128 else p


def kernel(n, ny, ids, table, mask_in, codes_in, spawn_in, survey_in, c_out, a_out, g_out,
           mask, codes, survey, load_sem, strips, tgt, s0, west, south, f0, cn, cs, cw, ce, f1, it, up, dl,
           s1, k1, b1, u1, v1, s2, k2, b2, u2, s3own, b3own, win,
           send_n, recv_n, send_g, recv_g):
    me = lax.axis_index("tile")
    n1, n2, n3 = ny // 2, ny // 4, ny // 8

    def guarded(d, body):
        ok = (me + d >= 0) & (me + d < n)
        pl.when(ok)(body)

    loads = [pltpu.make_async_copy(src, dst, load_sem.at[k]) for k, (src, dst) in enumerate(
        [(mask_in, mask), (codes_in, codes), (spawn_in, strips.at[2, 8:16]), (survey_in, survey)])]
    for load in loads:
        load.start()

    for lo in (0, 16):
        strips[:, lo:lo + 8, :] = jnp.zeros((3, 8, ny), f32)
    tgt[...] = jnp.zeros_like(tgt)
    for k in (0, 1):
        for lo in (0, 16):
            f1[k, lo:lo + 8] = jnp.zeros((8, 8, ny), f32)
    b2[...] = jnp.zeros_like(b2)
    win[...] = jnp.zeros_like(win)
    def loop(lo, hi, body):
        step = next(k for k in (4, 5, 3, 2, 1) if (hi - lo) % k == 0)

        def some(q, c):
            for k in range(step):
                body(lo + q * step + k)
            return c
        if hi - lo == step:
            some(0, 0)
        else:
            lax.fori_loop(0, (hi - lo) // step, some, 0)

    barrier = pltpu.get_barrier_semaphore()
    offsets = [d for k in range(1, REACH + 1) for d in (-k, k)]
    for d in offsets:
        guarded(d, lambda d=d: pl.semaphore_signal(
            barrier, inc=1, device_id={"tile": me + d}, device_id_type=pl.DeviceIdType.MESH))
    for load in loads[:3]:
        load.wait()
    strips[0, STRIP:2 * STRIP, :] = jnp.where(mask[...] > 0, 1.0, 0.0).astype(f32)
    strips[1, STRIP:2 * STRIP, :] = codes[...].astype(f32)

    def lanes(width):
        return lax.broadcasted_iota(jnp.int32, (8, width), 1)

    entries = lax.broadcasted_iota(jnp.int32, (8, table.shape[1]), 1)
    season = lax.broadcasted_iota(jnp.int32, (8, table.shape[1]), 0)
    wanted = jnp.full((8, table.shape[1]), ids[0], jnp.int32)
    for k in range(1, 8):
        wanted = jnp.where(season == k, ids[k], wanted)
    one = wanted == entries

    def pick(k):
        x = jnp.sum(jnp.where(one, table[k:k + 1, :], 0.0), axis=1, keepdims=True)
        return jnp.broadcast_to(x, (8, 128))
    mort, diff, strength = 0.03 * pick(0), pick(1), pick(4)
    u, v = 0.5 * pick(2), 0.5 * pick(3)
    diag = [mort + 4.0 * diff + u + v]
    diag += [4.0 ** l * mort + 4.0 * 2.0 ** l * diff for l in (1, 2, 3)]
    w = [0.8 / x for x in diag]
    g0, dd, uu, vv = w[0], w[0] * diff, w[0] * u, w[0] * v
    kappa = [2.0 ** l * diff * w[l] for l in range(4)]
    ratio = [diag[l] / diag[l + 1] for l in range(3)]

    def spread_row(r):
        s0[r] = jnp.broadcast_to(strips[0, r:r + 1, :], (8, ny))
        code = strips[1, r:r + 1, :]
        top = jnp.where(code >= 2.0, 1.0, 0.0)
        west[r] = jnp.broadcast_to(1.0 - (code - 2.0 * top), (8, ny))
        south[r] = jnp.broadcast_to(1.0 - top, (8, ny))
        f0[r] = s0[r] * wide(g0 * strength, ny) * jnp.broadcast_to(strips[2, r:r + 1, :], (8, ny))
    for r in range(8, 16):
        spread_row(r)

    def coefficients(adjoint, *ranges):
        D = wide(dd, ny)
        U = wide(uu, ny)
        V = wide(vv, ny)

        def row(r):
            lane = lanes(ny)
            s = s0[r]
            if adjoint:
                an, as_ = 1.0 - west[r - 1], west[r + 1]
                so = south[r]
                bw, be = 1.0 - pltpu.roll(so, 1, 1), pltpu.roll(so, ny - 1, 1)
            else:
                an, bw = west[r], south[r]
                as_, be = 1.0 - an, 1.0 - bw
            cn[r] = s * (D + U * an)
            cs[r] = s * (D + U * as_)
            cw[r] = jnp.where(lane == 0, 0.0, s * (D + V * bw))
            ce[r] = jnp.where(lane == ny - 1, 0.0, s * (D + V * be))
        for lo, hi in ranges:
            loop(lo, hi, row)

    pl.semaphore_wait(barrier, jnp.minimum(me, REACH) + jnp.minimum(n - 1 - me, REACH))

    def copy(src, dst, ssem, rsem, d):
        return pltpu.make_async_remote_copy(
            src_ref=src, dst_ref=dst, send_sem=ssem, recv_sem=rsem,
            device_id={"tile": me + d}, device_id_type=pl.DeviceIdType.MESH)

    pending = []

    def swap(k, up_src, up_dst, down_src, down_dst):
        def at(d):
            side = 0 if d < 0 else 1
            src, dst = (up_src, up_dst) if d < 0 else (down_src, down_dst)
            return copy(src, dst, send_n.at[k, side], recv_n.at[k, side], d)
        for d in (-1, 1):
            guarded(d, lambda d=d: at(d).start())
            pending.append((d, lambda d=d: at(d).wait_send()))

    def arrive(k, up_src, up_dst, down_src, down_dst):
        guarded(1, lambda: copy(up_src, up_dst, send_n.at[k, 0], recv_n.at[k, 0], 1).wait_recv())
        guarded(-1, lambda: copy(down_src, down_dst, send_n.at[k, 1], recv_n.at[k, 1], -1).wait_recv())

    def slot(k, i):
        return win.at[0, i, 1] if k == 0 else win.at[k, i]

    def gather_start(k, src):
        for d in offsets[::-1]:
            guarded(d, lambda d=d: copy(src, slot(k, REACH - d), send_g.at[k, REACH - d],
                                        recv_g.at[k, REACH - d], d).start())
            pending.append((d, lambda d=d: copy(
                src, slot(k, REACH - d), send_g.at[k, REACH - d],
                recv_g.at[k, REACH - d], d).wait_send()))

    def gather_wait(k, src):
        for d in offsets:
            guarded(d, lambda d=d: copy(src, slot(k, REACH + d), send_g.at[k, REACH + d],
                                        recv_g.at[k, REACH + d], d).wait_recv())

    ends = (strips.at[:, 8:16], strips.at[:, 16:24], strips.at[:, 8:16], strips.at[:, 0:8])
    swap(0, *ends)
    coefficients(False, (8, 16))
    arrive(0, *ends)
    for r in (*range(8), *range(16, 24)):
        spread_row(r)

    gi = lax.broadcasted_iota(jnp.int32, (256, 128), 0)
    gj = lax.broadcasted_iota(jnp.int32, (256, 128), 1)
    pair_sum = jnp.where(gi // 2 == gj, 1.0, 0.0).astype(bf16)
    hi_ = lax.broadcasted_iota(jnp.int32, (128, 256), 0)
    hj_ = lax.broadcasted_iota(jnp.int32, (128, 256), 1)
    spread = jnp.where(hj_ // 2 == hi_, 1.0, 0.0).astype(bf16)

    def times(x, m):
        big = x.astype(bf16)
        rest = (x - big.astype(f32)).astype(bf16)
        return (jnp.dot(big, m, preferred_element_type=f32)
                + jnp.dot(rest, m, preferred_element_type=f32))

    def restrict(src, lo, count, width):
        blocks = width // 256
        stack = []
        for i in range(count):
            x = src[lo + 2 * i] + src[lo + 2 * i + 1]
            stack += [x[:, b * 256:(b + 1) * 256] for b in range(blocks)]
        y = times(jnp.concatenate(stack, axis=0), pair_sum)
        rows = []
        for i in range(count):
            parts = [y[(i * blocks + b) * 8:(i * blocks + b + 1) * 8] for b in range(blocks)]
            rows.append(jnp.concatenate(parts, axis=1) if blocks > 1 else parts[0])
        return rows

    def prolong(rows):
        blocks = rows[0].shape[1] // 128
        stack = [x[:, b * 128:(b + 1) * 128] for x in rows for b in range(blocks)]
        y = times(jnp.concatenate(stack, axis=0), spread)
        out = []
        for i in range(len(rows)):
            parts = [y[(i * blocks + b) * 8:(i * blocks + b + 1) * 8] for b in range(blocks)]
            out.append(jnp.concatenate(parts, axis=1) if blocks > 1 else parts[0])
        return out

    def shifted(x):
        width = x.shape[1]
        lane = lanes(width)
        return (jnp.where(lane == 0, 0.0, pltpu.roll(x, 1, 1)),
                jnp.where(lane == width - 1, 0.0, pltpu.roll(x, width - 1, 1)))

    for i, x in enumerate(restrict(s0, 0, 12, ny)):
        s1[i] = jnp.where(x > 0.0, 1.0, 0.0)
        k1[i] = s1[i] * wide(kappa[1], n1)
    for i, x in enumerate(restrict(s1, 0, 6, n1)):
        s2[i] = jnp.where(x > 0.0, 1.0, 0.0)
        k2[i] = s2[i] * wide(kappa[2], n2)
    for i, x in enumerate(restrict(s2, 0, 3, n2)):
        s3own[i] = jnp.where(x > 0.0, 1.0, 0.0)
    gather_start(0, s3own.at[1])

    def relaxed0(f, r):
        x = f[r]
        return (0.2 * x + f0[r] + (cn[r] * f[r - 1] + cs[r] * f[r + 1])
                + (cw[r] * pltpu.roll(x, 1, 1) + ce[r] * pltpu.roll(x, ny - 1, 1)))

    def relaxed(f, b, k, r):
        x = f[r]
        w, e = shifted(x)
        return 0.2 * x + b[r] + k[r] * ((f[r - 1] + f[r + 1]) + (w + e))

    def coarse(k):
        inner = range(1, 2 * REACH)
        b = jnp.concatenate([win[k, i, 1] + (win[k, i - 1, 2] + win[k, i + 1, 0])
                             for i in inner], axis=0)
        weight = jnp.concatenate([win[0, i, 1] * kappa[3] for i in inner], axis=0)
        lane = lax.broadcasted_iota(jnp.int32, b.shape, 1)
        left = jnp.where(lane == 0, 0.0, weight)
        right = jnp.where(lane == n3 - 1, 0.0, weight)
        zero = jnp.zeros((8, n3), f32)
        x = b
        for _ in range(7):
            above = jnp.concatenate([zero, x[:-8]], axis=0)
            below = jnp.concatenate([x[8:], zero], axis=0)
            x = (0.2 * x + b + weight * (above + below)
                 + (left * pltpu.roll(x, 1, 1) + right * pltpu.roll(x, n3 - 1, 1)))
        mid = (REACH - 1) * 8
        return [x[mid - 8:mid], x[mid:mid + 8], x[mid + 8:mid + 16]]

    def below(f, turn, first_gather):
        for i, x in enumerate(restrict(dl, 4, 8, ny)):
            b1[2 + i] = x * wide(ratio[0], n1) * s1[2 + i]
        for r in range(4, 8):
            u1[r] = relaxed(b1, b1, k1, r) - b1[r]
        bb = b2.at[turn]
        for i, x in enumerate(restrict(u1, 4, 2, n1)):
            bb[2 + i] = x * wide(ratio[1], n2) * s2[2 + i]
        ends = (bb.at[2:4], bb.at[4:6], bb.at[2:4], bb.at[0:2])
        for r in (2, 3):
            x = bb[r]
            w, e = shifted(x)
            u2[r] = 0.2 * x + k2[r] * (bb[5 - r] + (w + e))
        zero = jnp.zeros((8, n2), f32)
        u2[0] = zero
        u2[1] = k2[1] * bb[2]
        u2[4] = k2[4] * bb[3]
        u2[5] = zero
        own = b3own.at[turn]
        for i, x in enumerate(restrict(u2, 0, 3, n2)):
            mine = x * ratio[2] * s3own[i]
            own[i] = mine
            win[1 + turn, REACH, i] = mine
        gather_start(1 + turn, own)
        swap(4 + turn, *ends)
        if first_gather:
            win[0, REACH, 1] = s3own[1]
            gather_wait(0, s3own.at[1])
        gather_wait(1 + turn, own)
        f3 = coarse(1 + turn)
        arrive(4 + turn, *ends)
        for i, x in enumerate(prolong(f3)):
            for j in (0, 1):
                r = 2 * i + j
                u2[r] = bb[r] + s2[r] * x
        f2 = [relaxed(u2, bb, k2, r) for r in range(1, 5)]
        for i, x in enumerate(prolong(f2)):
            for j in (0, 1):
                r = 2 + 2 * i + j
                u1[r] = b1[r] + s1[r] * x
        for r in range(3, 9):
            v1[r] = relaxed(u1, b1, k1, r)
        for i, x in enumerate(prolong([v1[r] for r in range(3, 9)])):
            for j in (0, 1):
                r = 6 + 2 * i + j
                up[r] = f[r] + s0[r] * x

    def solve(which, out, finish):
        turn = 2 * which

        def change(f, lo, hi):
            def row(r):
                dl[r] = relaxed0(f, r) - f[r]
            loop(lo, hi, row)
        change(f0, 4, 20)
        below(f0, turn, which == 0)
        second = f1.at[which]

        def first(r):
            second[r] = relaxed0(up, r)
        loop(7, 17, first)
        ends = (second.at[9:9 + HALO], second.at[17:17 + HALO],
                second.at[15 - HALO:15], second.at[7 - HALO:7])
        swap(1 + which, *ends)

        def again(r):
            it[r] = relaxed0(second, r)
        loop(8, 16, again)
        change(it, 9, 15)
        arrive(1 + which, *ends)
        loop(3, 8, again)
        loop(16, 21, again)
        change(it, 4, 9)
        change(it, 15, 20)
        below(it, turn + 1, False)
        for r in range(8):
            x = relaxed0(up, r + 8)
            out[r] = x
            finish(r, x)

    def to_target(r, x):
        misfit = jnp.sum(x, axis=0, keepdims=True) / 8.0 - survey[0, r:r + 1, :]
        tgt[8 + r:9 + r, :] = survey[1, r:r + 1, :] * misfit / 8.0

    def to_gradient(r, x):
        g_out[r:r + 1, :] = strips[0, 8 + r:9 + r, :] * jnp.sum(
            wide(strength, ny) * x, axis=0, keepdims=True)

    coefficients(False, (3, 8), (16, 21))
    loads[3].wait()
    solve(0, c_out, to_target)
    ends = (tgt.at[8:16], tgt.at[16:24], tgt.at[8:16], tgt.at[0:8])
    swap(3, *ends)
    coefficients(True, (3, 21))
    arrive(3, *ends)
    for r in range(24):
        f0[r] = s0[r] * wide(g0, ny) * jnp.broadcast_to(tgt[r:r + 1, :], (8, ny))
    solve(1, a_out, to_gradient)
    for d, wait in pending:
        guarded(d, wait)


def on_device(n, season_ids, season_table, shelf_mask, codes, spawn, survey):
    rows, ny = shelf_mask.shape
    fine = pltpu.VMEM((24, 8, ny), f32)
    lvl1 = pltpu.VMEM((12, 8, ny // 2), f32)
    lvl2 = pltpu.VMEM((6, 8, ny // 4), f32)
    slots = 2 * REACH + 1
    vm = pl.BlockSpec(memory_space=pltpu.VMEM)
    c, adj, g = pl.pallas_call(
        functools.partial(kernel, n, ny),
        out_shape=(jax.ShapeDtypeStruct((rows, 8, ny), f32),
                   jax.ShapeDtypeStruct((rows, 8, ny), f32),
                   jax.ShapeDtypeStruct((rows, ny), f32)),
        in_specs=[pl.BlockSpec(memory_space=pltpu.SMEM), vm] + [pl.BlockSpec(memory_space=pltpu.HBM)] * 4,
        out_specs=(vm, vm, vm),
        scratch_shapes=[
            pltpu.VMEM((rows, ny), jnp.int32), pltpu.VMEM((rows, ny), jnp.int32),
            pltpu.VMEM((2, rows, ny), f32), pltpu.SemaphoreType.DMA((4,)),
            pltpu.VMEM((3, 24, ny), f32), pltpu.VMEM((24, ny), f32),
            fine, fine, fine, fine, fine, fine, fine, fine,
            pltpu.VMEM((2, 24, 8, ny), f32), fine, fine, fine,
            lvl1, lvl1, lvl1, lvl1, lvl1, lvl2, lvl2,
            pltpu.VMEM((4, 6, 8, ny // 4), f32), lvl2,
            pltpu.VMEM((3, 8, ny // 8), f32), pltpu.VMEM((4, 3, 8, ny // 8), f32),
            pltpu.VMEM((5, slots, 3, 8, ny // 8), f32),
            pltpu.SemaphoreType.DMA((8, 2)), pltpu.SemaphoreType.DMA((8, 2)),
            pltpu.SemaphoreType.DMA((5, slots)), pltpu.SemaphoreType.DMA((5, slots)),
        ],
        compiler_params=pltpu.CompilerParams(
            collective_id=0, has_side_effects=True, vmem_limit_bytes=48 << 20),
        cost_estimate=pl.CostEstimate(flops=60_000_000, bytes_accessed=1_000_000, transcendentals=0),
    )(season_ids, season_table, shelf_mask, codes, spawn, survey)
    return jnp.transpose(c, (1, 0, 2)), jnp.transpose(adj, (1, 0, 2)), g


def solution(mesh):
    in_specs = (P("peel"), P(), P("tile", None), P("tile", None), P("tile", None),
                P("peel", "tile", None))
    out_specs = (P("peel", "tile", None), P("peel", "tile", None), P("tile", "peel"))
    return jax.shard_map(
        functools.partial(on_device, mesh.shape["tile"]), mesh=mesh,
        in_specs=in_specs, out_specs=out_specs, check_vma=False)
```
